32 devices in a mesh: groups: 2 (over x), rows: 16 (over z, y, core).
Axes of the slice: x: 2, y: 2, z: 4, core: 2. Of those that a mesh axis runs over, the one named last changes fastest.
Arguments:
- rhs: float32 [256, 128, 256], P(('groups', 'rows')), parts along dimension 0, may hold values from -6 to 6
- precision: float32 [256, 256], P(('groups', 'rows')), parts along dimension 0, may hold values from 0.25 to 4
- hessian: float32 [256, 256], P(('groups', 'rows')), parts along dimension 0, may hold values from 0.05 to 2
- diag_blocks: bfloat16 [256, 256, 256], P(('groups', 'rows')), parts along dimension 0, may hold values from -0.125 to 0.125
- cond_blocks: bfloat16 [256, 8, 256, 256], P(('groups', 'rows')), parts along dimension 0, may hold values from -0.125 to 0.125
- cond_ids: int32 [256, 8], P(('groups', 'rows')), parts along dimension 0, may hold values from 0 to 127, as said below
- step_alpha: float32 [2, 128], replicated, may hold values from 0.1 to 0.4
- step_beta: float32 [2, 128], replicated, may hold values from 0.2 to 0.8
Outputs:
- solution: float32 [256, 128, 256], P(('groups', 'rows')), parts along dimension 0
- residual: float32 [256, 128, 256], P(('groups', 'rows')), parts along dimension 0
- direction: float32 [256, 128, 256], P(('groups', 'rows')), parts along dimension 0
The draws below stay inside these ranges and needn't reach their ends.
There are 2 independent parts, one for each index of `groups`. The reference program is written for one: setup_inputs(seed, part) draws one part's arguments, and reference() takes and returns one part's arrays. A program takes and returns all parts, laid end to end along the dimension named above; an argument that names none is the same for every part. Nothing has to cross between parts.
Inputs may be any that keep to these rules, and one draw needn't show every extreme that they name: `cond_ids`: group the blocks into owner sets of 8 consecutive ones (owner set g holds blocks g * 8 onward; there are 128 / 8 owner sets, taken as a cycle). Each row lists 8 distinct blocks, none in its own owner set, all in owner sets at cycle distance 1 to 6 from its own. Over the rows of one owner set, at most 2 distinct blocks are listed from any other owner set, and exactly 2 from some.
All inputs are finite; a program needn't handle non-finite values.
Results may differ from the reference program's by a relative error of at most 0.0047.
Values may be sent and summed in bfloat16 or wider, within the bound.
A program may use at most 128 MiB of HBM per device.

```python
import math
import jax
import jax.numpy as jnp
from jax import lax

BS = 256
NCOND = 8
RADIUS = 6
ITERS = 2
BLK_DEV = 8
PROBES = 128
NBLK = 128


def draw_cond_ids(key, part):
    key = jax.random.fold_in(key, 7)
    dev_total = NBLK // BLK_DEV
    peer_max = 2 * RADIUS
    key_count, key_perm, key_first, key_second = jax.random.split(key, 4)
    signed_offsets = jnp.concatenate([jnp.arange(1, RADIUS + 1), -jnp.arange(1, RADIUS + 1)]).astype(jnp.int32)
    peer_count = jax.random.randint(key_count, (dev_total,), max(4, 2 * peer_max // 3), peer_max + 1)
    orders = jax.vmap(lambda single: jax.random.permutation(single, peer_max))(jax.random.split(key_perm, dev_total))
    offsets = jnp.take(signed_offsets, orders)
    owners = (jnp.arange(dev_total, dtype=jnp.int32)[:, None] + offsets + dev_total) % dev_total
    first_local = jax.random.randint(key_first, (dev_total, peer_max), 0, BLK_DEV)
    second_local = (first_local + jax.random.randint(key_second, (dev_total, peer_max), 1, BLK_DEV)) % BLK_DEV
    candidates = jnp.stack([owners * BLK_DEV + first_local, owners * BLK_DEV + second_local], axis=2)
    candidates = candidates.reshape(dev_total, 2 * peer_max)
    entry_index = jnp.arange(BLK_DEV * NCOND)[None, :] % (2 * peer_count[:, None])
    chosen = jnp.take_along_axis(candidates, entry_index, axis=1)
    return chosen.reshape(NBLK, NCOND).astype(jnp.int32)


def level_of(key, shape, cuts, smallest, largest):
    factor_of, own = 1.0, jax.random.fold_in(key, 6)
    for position, parts in cuts:
        steps = jnp.exp(jax.random.uniform(jax.random.fold_in(own, position), (parts,), jnp.float32, smallest / len(cuts), largest / len(cuts)))
        factor_of = factor_of * jnp.repeat(steps, shape[position] // parts).reshape([-1 if axis == position else 1 for axis in range(len(shape))])
    return factor_of


def scatter_about(own_key, shape, spread, reach, pieces=(), kind=jnp.bfloat16):
    drawn = spread * jax.random.normal(own_key, shape, jnp.float32)
    if pieces:
        drawn = drawn * level_of(own_key, shape, pieces, -0.22, 0.18)
    return jnp.clip(drawn, -reach, reach).astype(kind)


def setup_inputs(seed: int = 0, part: int = 0) -> dict:
    key_of = jax.random.split(jax.random.key(seed), 9)
    part_splits = jax.random.split(jax.random.fold_in(key_of[8], part), 9)
    return {
        "rhs": scatter_about(part_splits[0], (NBLK, PROBES, BS), 1.0, 6.0, ((0, 16),), jnp.float32),
        "precision": jnp.clip(jnp.exp(math.log(4.0) - 2.7725887 * jax.random.uniform(part_splits[1], (NBLK, BS), jnp.float32) ** level_of(part_splits[1], (NBLK, BS), ((0, 16),), -0.2, 0.2)), 0.25, 4.0),
        "hessian": jnp.clip(jnp.exp(math.log(2.0) - 3.6888794 * jax.random.uniform(part_splits[2], (NBLK, BS), jnp.float32) ** level_of(part_splits[2], (NBLK, BS), ((0, 16),), -0.2, 0.2)), 0.05, 2.0),
        "diag_blocks": scatter_about(part_splits[3], (NBLK, BS, BS), ((NCOND + 1) * BS) ** -0.5, 0.125, ((0, 16),)),
        "cond_blocks": scatter_about(part_splits[4], (NBLK, NCOND, BS, BS), ((NCOND + 1) * BS) ** -0.5, 0.125, ((0, 16),)),
        "cond_ids": draw_cond_ids(jax.random.fold_in(jax.random.fold_in(key_of[8], part), 71), part),
        "step_alpha": jnp.clip(jax.random.uniform(key_of[6], (ITERS, PROBES), jnp.float32, 0.1, 0.4), 0.1, 0.4),
        "step_beta": jnp.clip(jax.random.uniform(key_of[7], (ITERS, PROBES), jnp.float32, 0.2, 0.8), 0.2, 0.8),
    }


def reference(rhs, precision, hessian, diag_blocks, cond_blocks, cond_ids, step_alpha, step_beta):
    highest = lax.Precision.HIGHEST
    diag_wide = diag_blocks.astype(jnp.float32)

    def apply_operator(direction_now):
        probe_low = lax.optimization_barrier(direction_now.astype(jnp.bfloat16)).astype(jnp.float32)
        forward = jnp.einsum('bij,bpj->bpi', diag_wide, probe_low, precision=highest)
        for cond_slot in range(NCOND):
            factor = cond_blocks[:, cond_slot].astype(jnp.float32)
            picked = jnp.take(probe_low, cond_ids[:, cond_slot].astype(jnp.int32), axis=0)
            forward = forward + jnp.einsum('bij,bpj->bpi', factor, picked, precision=highest)
        scaled = lax.optimization_barrier((precision[:, None, :] * forward).astype(jnp.bfloat16)).astype(jnp.float32)
        back_image = jnp.einsum('bij,bpi->bpj', diag_wide, scaled, precision=highest)
        for cond_slot in range(NCOND):
            factor = cond_blocks[:, cond_slot].astype(jnp.float32)
            contrib = jnp.einsum('bij,bpi->bpj', factor, scaled, precision=highest)
            back_image = back_image.at[cond_ids[:, cond_slot].astype(jnp.int32)].add(contrib)
        return back_image + hessian[:, None, :] * direction_now

    solution = jnp.zeros_like(rhs)
    residual = rhs
    direction = rhs
    for iteration in range(ITERS):
        operator_image = apply_operator(direction)
        alpha_now = step_alpha[iteration][None, :, None]
        solution = solution + alpha_now * direction
        residual = residual - alpha_now * operator_image
        direction = residual + step_beta[iteration][None, :, None] * direction
    return solution, residual, direction
```

```python
import functools

import jax
import jax.numpy as jnp
from jax import lax
from jax.experimental import pallas as pl
from jax.experimental.pallas import tpu as pltpu
from jax.sharding import PartitionSpec as P

CAP = 2
RADIUS = 6
ITERS = 2
PEERS = 2 * RADIUS
MESH = pl.DeviceIdType.MESH

NT = (((1,), (1,)), ((), ()))
NN = (((1,), (0,)), ((), ()))


def offset_of(n):
    return (1 - 2 * (n % 2)) * (RADIUS - n // 2)


def kernel(
    dev_count, asked, entry, rhs, precision, hessian, alpha, beta, diag_hbm, cond_hbm,
    res_out, image_out,
    diag, cond, low, total, scaled, direc,
    pay, arr, ret, back,
    diag_sem, cond_sem, fsend, frecv, bsend, brecv,
):
    me = lax.axis_index("rows")
    own = rhs.shape[0]
    entries = cond_hbm.shape[0]

    def peer(n, sign):
        return lax.rem(me + sign * offset_of(n) + dev_count, dev_count)

    barrier = pltpu.get_barrier_semaphore()

    def greet(n, carry):
        pl.semaphore_signal(
            barrier, inc=1, device_id={"rows": peer(n, 1)}, device_id_type=MESH
        )
        return carry

    lax.fori_loop(0, PEERS, greet, 0)
    diag_copy = pltpu.make_async_copy(diag_hbm, diag, diag_sem)
    diag_copy.start()
    cond_copy = pltpu.make_async_copy(cond_hbm, cond.at[pl.ds(0, entries)], cond_sem)
    cond_copy.start()
    for b in range(own):
        low[b] = rhs[b].astype(jnp.bfloat16)
    cond[entries] = jnp.zeros(cond.shape[1:], cond.dtype)
    pl.semaphore_wait(barrier, PEERS)

    def fetch(t, n):
        return pltpu.make_async_remote_copy(
            src_ref=pay.at[t, n], dst_ref=arr.at[t, n],
            send_sem=fsend.at[t, n], recv_sem=frecv.at[t, n],
            device_id={"rows": peer(n, -1)}, device_id_type=MESH,
        )

    def give(t, n):
        return pltpu.make_async_remote_copy(
            src_ref=ret.at[t, n], dst_ref=back.at[t, n],
            send_sem=bsend.at[t, n], recv_sem=brecv.at[t, n],
            device_id={"rows": peer(n, 1)}, device_id_type=MESH,
        )

    for t in range(ITERS):
        def send_low(n, carry):
            for k in range(CAP):
                pay[t, n, k] = low[asked[n * CAP + k]]
            fetch(t, n).start()
            return carry

        lax.fori_loop(0, PEERS, send_low, 0)
        if t == 0:
            diag_copy.wait()

        def own_forward(b, carry):
            total[b] = lax.dot_general(low[b], diag[b], NT, preferred_element_type=jnp.float32)
            return carry

        lax.fori_loop(0, own, own_forward, 0)
        if t == 0:
            cond_copy.wait()

        def far_forward(n, carry):
            fetch(t, n).wait_recv()
            for b in range(own):
                acc = total[b]
                for k in range(CAP):
                    factor = cond[entry[(n * CAP + k) * own + b]]
                    acc = acc + lax.dot_general(
                        arr[t, n, k], factor, NT, preferred_element_type=jnp.float32
                    )
                total[b] = acc
            return carry

        lax.fori_loop(0, PEERS, far_forward, 0)
        for b in range(own):
            scaled[b] = (precision[b : b + 1, :] * total[b]).astype(jnp.bfloat16)

        def far_back(n, carry):
            for k in range(CAP):
                acc = jnp.zeros(total.shape[1:], jnp.float32)
                for b in range(own):
                    factor = cond[entry[(n * CAP + k) * own + b]]
                    acc = acc + lax.dot_general(
                        scaled[b], factor, NN, preferred_element_type=jnp.float32
                    )
                ret[t, n, k] = acc.astype(jnp.bfloat16)
            give(t, n).start()
            return carry

        lax.fori_loop(0, PEERS, far_back, 0)
        now = rhs if t == 0 else direc
        for b in range(own):
            image_out[b] = lax.dot_general(
                scaled[b], diag[b], NN, preferred_element_type=jnp.float32
            ) + hessian[b : b + 1, :] * now[b]

        def gather_back(n, carry):
            give(t, n).wait_recv()
            terms = [back[t, n, k].astype(jnp.float32) for k in range(CAP)]
            for b in range(own):
                acc = image_out[b]
                for k in range(CAP):
                    acc = acc + jnp.where(asked[n * CAP + k] == b, 1.0, 0.0) * terms[k]
                image_out[b] = acc
            return carry

        lax.fori_loop(0, PEERS, gather_back, 0)
        if t == 0:
            for b in range(own):
                left = rhs[b] - alpha[...] * image_out[b]
                res_out[b] = left
                new = left + beta[...] * rhs[b]
                direc[b] = new
                low[b] = new.astype(jnp.bfloat16)

    def drain(n, carry):
        for t in range(ITERS):
            fetch(t, n).wait_send()
            give(t, n).wait_send()
        return carry

    lax.fori_loop(0, PEERS, drain, 0)


def two_blocks(lists, owner, own):
    hit = lists // own == owner
    local = lists % own
    return (
        jnp.min(jnp.where(hit, local, own), axis=1),
        jnp.max(jnp.where(hit, local, -1), axis=1),
    )


def on_device(rhs, precision, hessian, diag_blocks, cond_blocks, cond_ids, step_alpha, step_beta):
    dev_count = lax.axis_size("rows")
    me = lax.axis_index("rows")
    own, probes, points = rhs.shape
    conds = cond_ids.shape[1]
    entries = own * conds
    flat = cond_ids.reshape(1, entries)
    everyone = lax.all_gather(flat[0], "rows")
    offsets = jnp.array([offset_of(n) for n in range(PEERS)], jnp.int32)
    owners = (me + offsets + dev_count) % dev_count
    listers = (me - offsets + dev_count) % dev_count

    lo, hi = two_blocks(flat, owners[:, None], own)
    second = jnp.where(hi > lo, hi, -1)
    local = jnp.stack([jnp.where(lo < own, lo, -1), second], axis=1)
    wanted = jnp.where(local >= 0, owners[:, None] * own + local, -1)
    same = wanted[:, :, None, None] == cond_ids[None, None, :, :]
    number = jnp.arange(entries, dtype=jnp.int32).reshape(own, conds)
    entry = jnp.min(jnp.where(same, number, entries), axis=3).reshape(-1)

    their_lo, their_hi = two_blocks(jnp.take(everyone, listers, axis=0), me, own)
    asked = jnp.stack([their_lo % own, jnp.maximum(their_hi, 0)], axis=1).reshape(-1)

    alpha0 = step_alpha[0][:, None]
    beta0 = step_beta[0][:, None]
    vmem = pl.BlockSpec(memory_space=pltpu.VMEM)
    smem = pl.BlockSpec(memory_space=pltpu.SMEM)
    hbm = pl.BlockSpec(memory_space=pl.ANY)
    low_type = jnp.bfloat16
    slots = (ITERS, PEERS, CAP, probes, points)
    res1, image1 = pl.pallas_call(
        functools.partial(kernel, dev_count),
        out_shape=[jax.ShapeDtypeStruct(rhs.shape, jnp.float32)] * 2,
        in_specs=[smem, smem, vmem, vmem, vmem, vmem, vmem, hbm, hbm],
        out_specs=[vmem, vmem],
        scratch_shapes=[
            pltpu.VMEM(diag_blocks.shape, low_type),
            pltpu.VMEM((entries + 1, points, points), low_type),
            pltpu.VMEM(rhs.shape, low_type),
            pltpu.VMEM(rhs.shape, jnp.float32),
            pltpu.VMEM(rhs.shape, low_type),
            pltpu.VMEM(rhs.shape, jnp.float32),
            pltpu.VMEM(slots, low_type),
            pltpu.VMEM(slots, low_type),
            pltpu.VMEM(slots, low_type),
            pltpu.VMEM(slots, low_type),
            pltpu.SemaphoreType.DMA,
            pltpu.SemaphoreType.DMA,
            pltpu.SemaphoreType.DMA((ITERS, PEERS)),
            pltpu.SemaphoreType.DMA((ITERS, PEERS)),
            pltpu.SemaphoreType.DMA((ITERS, PEERS)),
            pltpu.SemaphoreType.DMA((ITERS, PEERS)),
        ],
        compiler_params=pltpu.CompilerParams(
            collective_id=0, has_side_effects=True, vmem_limit_bytes=48 * 1024 * 1024
        ),
    )(
        asked, entry, rhs, precision, hessian, alpha0, beta0,
        diag_blocks, cond_blocks.reshape(entries, points, points),
    )
    alpha1 = step_alpha[1][None, :, None]
    beta1 = step_beta[1][None, :, None]
    dir1 = res1 + beta0[None] * rhs
    sol = alpha0[None] * rhs + alpha1 * dir1
    res = res1 - alpha1 * image1
    return (sol, res, res + beta1 * dir1)


def solution(mesh):
    in_specs = (
        P(("groups", "rows"), None, None),
        P(("groups", "rows"), None),
        P(("groups", "rows"), None),
        P(("groups", "rows"), None, None),
        P(("groups", "rows"), None, None, None),
        P(("groups", "rows"), None),
        P(),
        P(),
    )
    out_specs = (
        P(("groups", "rows"), None, None),
        P(("groups", "rows"), None, None),
        P(("groups", "rows"), None, None),
    )
    return jax.shard_map(
        on_device, mesh=mesh, in_specs=in_specs, out_specs=out_specs, check_vma=False
    )
```

```python
import functools

import jax
import jax.numpy as jnp
from jax import lax
from jax.experimental import pallas as pl
from jax.experimental.pallas import tpu as pltpu
from jax.sharding import PartitionSpec as P

CAP = 2
RADIUS = 6
ITERS = 2
PEERS = 2 * RADIUS
MESH = pl.DeviceIdType.MESH

NT = (((1,), (1,)), ((), ()))
NN = (((1,), (0,)), ((), ()))


def offset_of(n):
    return (1 - 2 * (n % 2)) * (RADIUS - n // 2)


def kernel(
    dev_count, ids, alpha_rows, beta_rows,
    rhs_hbm, precision_hbm, hessian_hbm, diag_hbm, cond_hbm,
    res_out, image_out,
    rhs, precision, hessian, diag, cond, low, total, scaled, direc, alpha, beta,
    want, got, entry_rows, got_smem, entry_smem,
    pay, arr, ret, back,
    local_sem, smem_sem, wsend, wrecv, fsend, frecv, bsend, brecv,
):
    me = lax.axis_index("rows")
    own, probes, points = rhs.shape
    entries = cond_hbm.shape[0]
    conds = entries // own

    def peer(n, sign):
        return lax.rem(me + sign * offset_of(n) + dev_count, dev_count)

    barrier = pltpu.get_barrier_semaphore()

    def greet(n, carry):
        pl.semaphore_signal(
            barrier, inc=1, device_id={"rows": peer(n, 1)}, device_id_type=MESH
        )
        return carry

    lax.fori_loop(0, PEERS, greet, 0)
    pairs = [
        (rhs_hbm, rhs), (precision_hbm, precision), (hessian_hbm, hessian), (diag_hbm, diag),
        (cond_hbm, cond.at[pl.ds(0, entries)]),
    ]
    loads = [
        pltpu.make_async_copy(source, target, local_sem.at[number])
        for number, (source, target) in enumerate(pairs)
    ]
    for load in loads:
        load.start()

    lane = lax.broadcasted_iota(jnp.int32, (16, 128), 1)
    slot = lax.broadcasted_iota(jnp.int32, (16, 128), 0)
    distance = (1 - 2 * (slot & 1)) * (RADIUS - (slot >> 1))
    owner = me + distance
    owner = jnp.where(owner < 0, owner + dev_count, owner)
    owner = jnp.where(owner >= dev_count, owner - dev_count, owner)
    listed = ids[0:1, :] - owner * own
    hit = (listed >= 0) & (listed < own)
    lowest = jnp.min(jnp.where(hit, listed, own), axis=1, keepdims=True)
    highest = jnp.max(jnp.where(hit, listed, -1), axis=1, keepdims=True)
    first = jnp.where(lowest < own, lowest, -1)
    second = jnp.where(highest > lowest, highest, -1)
    rows = jnp.where(lane == 0, first, jnp.where(lane == 1, second, 0))
    for n in range(PEERS):
        want[n] = rows[n : n + 1, :]
    pl.semaphore_wait(barrier, PEERS)

    def tell(n):
        return pltpu.make_async_remote_copy(
            src_ref=want.at[n], dst_ref=got.at[n],
            send_sem=wsend.at[n], recv_sem=wrecv.at[n],
            device_id={"rows": peer(n, 1)}, device_id_type=MESH,
        )

    def start_tell(n, carry):
        tell(n).start()
        return carry

    def wait_tell(n, carry):
        tell(n).wait_recv()
        return carry

    lax.fori_loop(0, PEERS, start_tell, 0)
    loads[0].wait()
    for b in range(own):
        low[b] = rhs[b].astype(jnp.bfloat16)
    lax.fori_loop(0, PEERS, wait_tell, 0)
    asked_copy = pltpu.make_async_copy(got, got_smem, smem_sem.at[0])
    asked_copy.start()
    asked_copy.wait()

    def asked(n, k):
        return got_smem[n, 0, k]

    def entry(n, k, b):
        return entry_smem[n * CAP + k, 0, b]

    def prepare():
        column = lax.broadcasted_iota(jnp.int32, (conds, 128), 1)
        number = column * conds + lax.broadcasted_iota(jnp.int32, (conds, 128), 0)
        by_row = ids[8 : 8 + conds, :]
        for n in range(PEERS):
            base = owner[n : n + 1, :] * own
            for k, local in enumerate((first, second)):
                mine = local[n : n + 1, :]
                block = jnp.where(mine >= 0, base + mine, -2)
                found = jnp.where((by_row == block) & (column < own), number, entries)
                entry_rows[n * CAP + k] = jnp.min(found, axis=0, keepdims=True)
        entry_copy = pltpu.make_async_copy(entry_rows, entry_smem, smem_sem.at[1])
        entry_copy.start()
        for rows_ref, full in ((alpha_rows, alpha), (beta_rows, beta)):
            spread = jnp.transpose(jnp.broadcast_to(rows_ref[0:1, :], (128, probes)))
            for part in range(points // 128):
                full[:, part * 128 : (part + 1) * 128] = spread
        cond[entries] = jnp.zeros(cond.shape[1:], cond.dtype)
        for load in loads[1:4]:
            load.wait()
        entry_copy.wait()

    def fetch(t, n):
        return pltpu.make_async_remote_copy(
            src_ref=pay.at[t, n], dst_ref=arr.at[t, n],
            send_sem=fsend.at[t, n], recv_sem=frecv.at[t, n],
            device_id={"rows": peer(n, -1)}, device_id_type=MESH,
        )

    def give(t, n):
        return pltpu.make_async_remote_copy(
            src_ref=ret.at[t, n], dst_ref=back.at[t, n],
            send_sem=bsend.at[t, n], recv_sem=brecv.at[t, n],
            device_id={"rows": peer(n, 1)}, device_id_type=MESH,
        )

    for t in range(ITERS):
        def send_low(n, carry):
            for k in range(CAP):
                pay[t, n, k] = low[jnp.maximum(asked(n, k), 0)]
            fetch(t, n).start()
            return carry

        lax.fori_loop(0, PEERS, send_low, 0)
        if t == 0:
            prepare()

        def own_forward(b, carry):
            total[b] = lax.dot_general(low[b], diag[b], NT, preferred_element_type=jnp.float32)
            return carry

        lax.fori_loop(0, own, own_forward, 0)
        if t == 0:
            loads[4].wait()

        def far_forward(n, carry):
            fetch(t, n).wait_recv()
            for b in range(own):
                acc = total[b]
                for k in range(CAP):
                    factor = cond[entry(n, k, b)]
                    acc = acc + lax.dot_general(
                        arr[t, n, k], factor, NT, preferred_element_type=jnp.float32
                    )
                total[b] = acc
            return carry

        lax.fori_loop(0, PEERS, far_forward, 0)
        for b in range(own):
            scaled[b] = (precision[b : b + 1, :] * total[b]).astype(jnp.bfloat16)

        def far_back(n, carry):
            for k in range(CAP):
                acc = jnp.zeros(total.shape[1:], jnp.float32)
                for b in range(own):
                    factor = cond[entry(n, k, b)]
                    acc = acc + lax.dot_general(
                        scaled[b], factor, NN, preferred_element_type=jnp.float32
                    )
                ret[t, n, k] = acc.astype(jnp.bfloat16)
            give(t, n).start()
            return carry

        lax.fori_loop(0, PEERS, far_back, 0)
        now = rhs if t == 0 else direc
        for b in range(own):
            image_out[b] = lax.dot_general(
                scaled[b], diag[b], NN, preferred_element_type=jnp.float32
            ) + hessian[b : b + 1, :] * now[b]

        def gather_back(n, carry):
            give(t, n).wait_recv()
            terms = [back[t, n, k].astype(jnp.float32) for k in range(CAP)]
            for b in range(own):
                acc = image_out[b]
                for k in range(CAP):
                    acc = acc + jnp.where(asked(n, k) == b, 1.0, 0.0) * terms[k]
                image_out[b] = acc
            return carry

        lax.fori_loop(0, PEERS, gather_back, 0)
        if t == 0:
            for b in range(own):
                left = rhs[b] - alpha[...] * image_out[b]
                res_out[b] = left
                new = left + beta[...] * rhs[b]
                direc[b] = new
                low[b] = new.astype(jnp.bfloat16)

    def drain(n, carry):
        tell(n).wait_send()
        for t in range(ITERS):
            fetch(t, n).wait_send()
            give(t, n).wait_send()
        return carry

    lax.fori_loop(0, PEERS, drain, 0)


def on_device(rhs, precision, hessian, diag_blocks, cond_blocks, cond_ids, step_alpha, step_beta):
    dev_count = lax.axis_size("rows")
    own, probes, points = rhs.shape
    conds = cond_ids.shape[1]
    entries = own * conds
    flat = jnp.pad(cond_ids.reshape(1, entries), ((0, 7), (0, 128 - entries)), constant_values=-1)
    by_row = jnp.pad(cond_ids.T, ((0, 0), (0, 128 - own)), constant_values=-1)
    ids = jnp.concatenate([flat, by_row], axis=0)
    vmem = pl.BlockSpec(memory_space=pltpu.VMEM)
    hbm = pl.BlockSpec(memory_space=pl.ANY)
    low_type = jnp.bfloat16
    slots = (ITERS, PEERS, CAP, probes, points)
    res1, image1 = pl.pallas_call(
        functools.partial(kernel, dev_count),
        out_shape=[jax.ShapeDtypeStruct(rhs.shape, jnp.float32)] * 2,
        in_specs=[vmem] * 3 + [hbm] * 5,
        out_specs=[vmem, vmem],
        scratch_shapes=[
            pltpu.VMEM(rhs.shape, jnp.float32),
            pltpu.VMEM(precision.shape, jnp.float32),
            pltpu.VMEM(hessian.shape, jnp.float32),
            pltpu.VMEM(diag_blocks.shape, low_type),
            pltpu.VMEM((entries + 1, points, points), low_type),
            pltpu.VMEM(rhs.shape, low_type),
            pltpu.VMEM(rhs.shape, jnp.float32),
            pltpu.VMEM(rhs.shape, low_type),
            pltpu.VMEM(rhs.shape, jnp.float32),
            pltpu.VMEM((probes, points), jnp.float32),
            pltpu.VMEM((probes, points), jnp.float32),
            pltpu.VMEM((PEERS, 1, 128), jnp.int32),
            pltpu.VMEM((PEERS, 1, 128), jnp.int32),
            pltpu.VMEM((PEERS * CAP, 1, 128), jnp.int32),
            pltpu.SMEM((PEERS, 1, 128), jnp.int32),
            pltpu.SMEM((PEERS * CAP, 1, 128), jnp.int32),
            pltpu.VMEM(slots, low_type),
            pltpu.VMEM(slots, low_type),
            pltpu.VMEM(slots, low_type),
            pltpu.VMEM(slots, low_type),
            pltpu.SemaphoreType.DMA((5,)),
            pltpu.SemaphoreType.DMA((2,)),
            pltpu.SemaphoreType.DMA((PEERS,)),
            pltpu.SemaphoreType.DMA((PEERS,)),
            pltpu.SemaphoreType.DMA((ITERS, PEERS)),
            pltpu.SemaphoreType.DMA((ITERS, PEERS)),
            pltpu.SemaphoreType.DMA((ITERS, PEERS)),
            pltpu.SemaphoreType.DMA((ITERS, PEERS)),
        ],
        compiler_params=pltpu.CompilerParams(
            collective_id=0, has_side_effects=True, vmem_limit_bytes=56 * 1024 * 1024
        ),
    )(
        ids, step_alpha, step_beta, rhs, precision, hessian, diag_blocks,
        cond_blocks.reshape(entries, points, points),
    )
    alpha0 = step_alpha[0][None, :, None]
    beta0 = step_beta[0][None, :, None]
    alpha1 = step_alpha[1][None, :, None]
    beta1 = step_beta[1][None, :, None]
    dir1 = res1 + beta0 * rhs
    sol = alpha0 * rhs + alpha1 * dir1
    res = res1 - alpha1 * image1
    return (sol, res, res + beta1 * dir1)


def solution(mesh):
    in_specs = (
        P(("groups", "rows"), None, None),
        P(("groups", "rows"), None),
        P(("groups", "rows"), None),
        P(("groups", "rows"), None, None),
        P(("groups", "rows"), None, None, None),
        P(("groups", "rows"), None),
        P(),
        P(),
    )
    out_specs = (
        P(("groups", "rows"), None, None),
        P(("groups", "rows"), None, None),
        P(("groups", "rows"), None, None),
    )
    return jax.shard_map(
        on_device, mesh=mesh, in_specs=in_specs, out_specs=out_specs, check_vma=False
    )
```

```python
import functools

import jax
import jax.numpy as jnp
from jax import lax
from jax.experimental import pallas as pl
from jax.experimental.pallas import tpu as pltpu
from jax.sharding import PartitionSpec as P

CAP = 2
RADIUS = 6
ITERS = 2
PEERS = 2 * RADIUS
MESH = pl.DeviceIdType.MESH

NT = (((1,), (1,)), ((), ()))
NN = (((1,), (0,)), ((), ()))


def offset_of(n):
    return (1 - 2 * (n % 2)) * (RADIUS * (1 - n // 2 % 2) + n // 2 % 2 + (2 * (n // 2 % 2) - 1) * (n // 4))


def kernel(
    dev_count, ids, alpha_rows, beta_rows,
    rhs_hbm, precision_hbm, hessian_hbm, diag_hbm, cond_hbm,
    res_out, image_out,
    rhs, precision, hessian, diag, cond, low, total, scaled, direc, alpha, beta,
    want, got, entry_rows, got_smem, entry_smem,
    pay, arr, ret, back,
    local_sem, smem_sem, wsend, wrecv, fsend, frecv, bsend, brecv,
):
    me = lax.axis_index("rows")
    own, probes, points = rhs.shape
    entries = cond_hbm.shape[0]
    conds = entries // own

    def peer(n, sign):
        return lax.rem(me + sign * offset_of(n) + dev_count, dev_count)

    barrier = pltpu.get_barrier_semaphore()

    def greet(n, carry):
        pl.semaphore_signal(
            barrier, inc=1, device_id={"rows": peer(n, 1)}, device_id_type=MESH
        )
        return carry

    lax.fori_loop(0, PEERS, greet, 0)
    pairs = [
        (rhs_hbm, rhs), (precision_hbm, precision), (hessian_hbm, hessian), (diag_hbm, diag),
        (cond_hbm, cond.at[pl.ds(0, entries)]),
    ]
    loads = [
        pltpu.make_async_copy(source, target, local_sem.at[number])
        for number, (source, target) in enumerate(pairs)
    ]
    for load in loads:
        load.start()

    lane = lax.broadcasted_iota(jnp.int32, (1, 128), 1)
    chosen = []
    for n in range(PEERS):
        base = peer(n, 1) * own
        listed = ids[...] - base
        hit = (listed >= 0) & (listed < own)
        lowest = jnp.min(jnp.where(hit, listed, own), axis=(0, 1), keepdims=True)
        highest = jnp.max(jnp.where(hit, listed, -1), axis=(0, 1), keepdims=True)
        first = jnp.where(lowest < own, lowest, -1)
        second = jnp.where(highest > lowest, highest, -1)
        chosen.append((base, first, second))
        want[n] = jnp.where(lane == 0, first, jnp.where(lane == 1, second, 0))
    pl.semaphore_wait(barrier, PEERS)

    def tell(n):
        return pltpu.make_async_remote_copy(
            src_ref=want.at[n], dst_ref=got.at[n],
            send_sem=wsend.at[n], recv_sem=wrecv.at[n],
            device_id={"rows": peer(n, 1)}, device_id_type=MESH,
        )

    def start_tell(n, carry):
        tell(n).start()
        return carry

    def wait_tell(n, carry):
        tell(n).wait_recv()
        return carry

    lax.fori_loop(0, PEERS, start_tell, 0)
    loads[0].wait()
    for b in range(own):
        low[b] = rhs[b].astype(jnp.bfloat16)
    lax.fori_loop(0, PEERS, wait_tell, 0)
    asked_copy = pltpu.make_async_copy(got, got_smem, smem_sem.at[0])
    asked_copy.start()
    asked_copy.wait()

    def asked(n, k):
        return got_smem[n, 0, k]

    def entry(n, k, b):
        return entry_smem[b, n * CAP + k]

    def prepare():
        number = lax.broadcasted_iota(jnp.int32, (own, conds), 0) * conds
        number = number + lax.broadcasted_iota(jnp.int32, (own, conds), 1)
        column = lax.broadcasted_iota(jnp.int32, (own, 128), 1)
        table = jnp.full((own, 128), entries, jnp.int32)
        for n, (base, *locals_) in enumerate(chosen):
            for k, mine in enumerate(locals_):
                block = jnp.where(mine >= 0, base + mine, -2)
                found = jnp.where(ids[...] == block, number, entries)
                least = jnp.min(found, axis=1, keepdims=True)
                table = jnp.where(column == n * CAP + k, least, table)
        entry_rows[...] = table
        entry_copy = pltpu.make_async_copy(entry_rows, entry_smem, smem_sem.at[1])
        entry_copy.start()
        for rows_ref, full in ((alpha_rows, alpha), (beta_rows, beta)):
            spread = jnp.transpose(jnp.broadcast_to(rows_ref[0:1, :], (128, probes)))
            for part in range(points // 128):
                full[:, part * 128 : (part + 1) * 128] = spread
        cond[entries] = jnp.zeros(cond.shape[1:], cond.dtype)
        for load in loads[1:4]:
            load.wait()
        entry_copy.wait()

    def fetch(t, n):
        return pltpu.make_async_remote_copy(
            src_ref=pay.at[t, n], dst_ref=arr.at[t, n],
            send_sem=fsend.at[t, n], recv_sem=frecv.at[t, n],
            device_id={"rows": peer(n, -1)}, device_id_type=MESH,
        )

    def give(t, n):
        return pltpu.make_async_remote_copy(
            src_ref=ret.at[t, n], dst_ref=back.at[t, n],
            send_sem=bsend.at[t, n], recv_sem=brecv.at[t, n],
            device_id={"rows": peer(n, 1)}, device_id_type=MESH,
        )

    for t in range(ITERS):
        def send_low(n, carry):
            for k in range(CAP):
                pay[t, n, k] = low[jnp.maximum(asked(n, k), 0)]
            fetch(t, n).start()
            return carry

        lax.fori_loop(0, PEERS, send_low, 0)
        if t == 0:
            prepare()

        def own_forward(b, carry):
            total[b] = lax.dot_general(low[b], diag[b], NT, preferred_element_type=jnp.float32)
            return carry

        lax.fori_loop(0, own, own_forward, 0)
        if t == 0:
            loads[4].wait()

        def far_forward(n, carry):
            fetch(t, n).wait_recv()
            for b in range(own):
                acc = total[b]
                for k in range(CAP):
                    factor = cond[entry(n, k, b)]
                    acc = acc + lax.dot_general(
                        arr[t, n, k], factor, NT, preferred_element_type=jnp.float32
                    )
                total[b] = acc
            return carry

        lax.fori_loop(0, PEERS, far_forward, 0)
        for b in range(own):
            scaled[b] = (precision[b : b + 1, :] * total[b]).astype(jnp.bfloat16)

        def far_back(n, carry):
            for k in range(CAP):
                acc = jnp.zeros(total.shape[1:], jnp.float32)
                for b in range(own):
                    factor = cond[entry(n, k, b)]
                    acc = acc + lax.dot_general(
                        scaled[b], factor, NN, preferred_element_type=jnp.float32
                    )
                ret[t, n, k] = acc.astype(jnp.bfloat16)
            give(t, n).start()
            return carry

        lax.fori_loop(0, PEERS, far_back, 0)
        now = rhs if t == 0 else direc
        for b in range(own):
            image_out[b] = lax.dot_general(
                scaled[b], diag[b], NN, preferred_element_type=jnp.float32
            ) + hessian[b : b + 1, :] * now[b]

        def gather_back(n, carry):
            give(t, n).wait_recv()
            terms = [back[t, n, k].astype(jnp.float32) for k in range(CAP)]
            for b in range(own):
                acc = image_out[b]
                for k in range(CAP):
                    acc = acc + jnp.where(asked(n, k) == b, 1.0, 0.0) * terms[k]
                image_out[b] = acc
            return carry

        lax.fori_loop(0, PEERS, gather_back, 0)
        if t == 0:
            for b in range(own):
                left = rhs[b] - alpha[...] * image_out[b]
                res_out[b] = left
                new = left + beta[...] * rhs[b]
                direc[b] = new
                low[b] = new.astype(jnp.bfloat16)

    def drain(n, carry):
        tell(n).wait_send()
        for t in range(ITERS):
            fetch(t, n).wait_send()
            give(t, n).wait_send()
        return carry

    lax.fori_loop(0, PEERS, drain, 0)


def on_device(rhs, precision, hessian, diag_blocks, cond_blocks, cond_ids, step_alpha, step_beta):
    dev_count = lax.axis_size("rows")
    own, probes, points = rhs.shape
    conds = cond_ids.shape[1]
    entries = own * conds
    vmem = pl.BlockSpec(memory_space=pltpu.VMEM)
    hbm = pl.BlockSpec(memory_space=pl.ANY)
    low_type = jnp.bfloat16
    slots = (ITERS, PEERS, CAP, probes, points)
    res1, image1 = pl.pallas_call(
        functools.partial(kernel, dev_count),
        out_shape=[jax.ShapeDtypeStruct(rhs.shape, jnp.float32)] * 2,
        in_specs=[vmem] * 3 + [hbm] * 5,
        out_specs=[vmem, vmem],
        scratch_shapes=[
            pltpu.VMEM(rhs.shape, jnp.float32),
            pltpu.VMEM(precision.shape, jnp.float32),
            pltpu.VMEM(hessian.shape, jnp.float32),
            pltpu.VMEM(diag_blocks.shape, low_type),
            pltpu.VMEM((entries + 1, points, points), low_type),
            pltpu.VMEM(rhs.shape, low_type),
            pltpu.VMEM(rhs.shape, jnp.float32),
            pltpu.VMEM(rhs.shape, low_type),
            pltpu.VMEM(rhs.shape, jnp.float32),
            pltpu.VMEM((probes, points), jnp.float32),
            pltpu.VMEM((probes, points), jnp.float32),
            pltpu.VMEM((PEERS, 1, 128), jnp.int32),
            pltpu.VMEM((PEERS, 1, 128), jnp.int32),
            pltpu.VMEM((own, 128), jnp.int32),
            pltpu.SMEM((PEERS, 1, 128), jnp.int32),
            pltpu.SMEM((own, 128), jnp.int32),
            pltpu.VMEM(slots, low_type),
            pltpu.VMEM(slots, low_type),
            pltpu.VMEM(slots, low_type),
            pltpu.VMEM(slots, low_type),
            pltpu.SemaphoreType.DMA((5,)),
            pltpu.SemaphoreType.DMA((2,)),
            pltpu.SemaphoreType.DMA((PEERS,)),
            pltpu.SemaphoreType.DMA((PEERS,)),
            pltpu.SemaphoreType.DMA((ITERS, PEERS)),
            pltpu.SemaphoreType.DMA((ITERS, PEERS)),
            pltpu.SemaphoreType.DMA((ITERS, PEERS)),
            pltpu.SemaphoreType.DMA((ITERS, PEERS)),
        ],
        compiler_params=pltpu.CompilerParams(
            collective_id=0, has_side_effects=True, vmem_limit_bytes=56 * 1024 * 1024
        ),
    )(
        cond_ids, step_alpha, step_beta, rhs, precision, hessian, diag_blocks,
        cond_blocks.reshape(entries, points, points),
    )
    alpha0 = step_alpha[0][None, :, None]
    beta0 = step_beta[0][None, :, None]
    alpha1 = step_alpha[1][None, :, None]
    beta1 = step_beta[1][None, :, None]
    dir1 = res1 + beta0 * rhs
    sol = alpha0 * rhs + alpha1 * dir1
    res = res1 - alpha1 * image1
    return (sol, res, res + beta1 * dir1)


def solution(mesh):
    in_specs = (
        P(("groups", "rows"), None, None),
        P(("groups", "rows"), None),
        P(("groups", "rows"), None),
        P(("groups", "rows"), None, None),
        P(("groups", "rows"), None, None, None),
        P(("groups", "rows"), None),
        P(),
        P(),
    )
    out_specs = (
        P(("groups", "rows"), None, None),
        P(("groups", "rows"), None, None),
        P(("groups", "rows"), None, None),
    )
    return jax.shard_map(
        on_device, mesh=mesh, in_specs=in_specs, out_specs=out_specs, check_vma=False
    )
```

```python
import functools

import jax
import jax.numpy as jnp
from jax import lax
from jax.experimental import pallas as pl
from jax.experimental.pallas import tpu as pltpu
from jax.sharding import PartitionSpec as P

CAP = 2
RADIUS = 6
ITERS = 2
PEERS = 2 * RADIUS
MESH = pl.DeviceIdType.MESH

NT = (((1,), (1,)), ((), ()))
NN = (((1,), (0,)), ((), ()))


def offset_of(n):
    return (1 - 2 * (n % 2)) * (RADIUS * (1 - n // 2 % 2) + n // 2 % 2 + (2 * (n // 2 % 2) - 1) * (n // 4))


def kernel(
    dev_count, ids, alpha_rows, beta_rows,
    rhs_hbm, precision_hbm, hessian_hbm, diag_hbm, cond_hbm,
    res_out, image_out,
    rhs, precision, hessian, diag, cond, low, total, scaled, direc, alpha, beta,
    want, got, entry_rows, got_smem, entry_smem,
    pay, arr, ret, back,
    local_sem, smem_sem, wsend, wrecv, fsend, frecv, bsend, brecv,
):
    me = lax.axis_index("rows")
    own, probes, points = rhs.shape
    entries = cond_hbm.shape[0]
    conds = entries // own

    def peer(n, sign):
        return lax.rem(me + sign * offset_of(n) + dev_count, dev_count)

    barrier = pltpu.get_barrier_semaphore()

    def greet(n, carry):
        pl.semaphore_signal(
            barrier, inc=1, device_id={"rows": peer(n, 1)}, device_id_type=MESH
        )
        return carry

    lax.fori_loop(0, PEERS, greet, 0)
    pairs = [
        (rhs_hbm, rhs), (precision_hbm, precision), (hessian_hbm, hessian), (diag_hbm, diag),
        (cond_hbm, cond.at[pl.ds(0, entries)]),
    ]
    loads = [
        pltpu.make_async_copy(source, target, local_sem.at[number])
        for number, (source, target) in enumerate(pairs)
    ]
    for load in loads:
        load.start()

    lane = lax.broadcasted_iota(jnp.int32, (1, 128), 1)
    chosen = []
    for n in range(PEERS):
        base = peer(n, 1) * own
        listed = ids[...] - base
        hit = (listed >= 0) & (listed < own)
        lowest = jnp.min(jnp.where(hit, listed, own), axis=(0, 1), keepdims=True)
        highest = jnp.max(jnp.where(hit, listed, -1), axis=(0, 1), keepdims=True)
        first = jnp.where(lowest < own, lowest, -1)
        second = jnp.where(highest > lowest, highest, -1)
        chosen.append((base, first, second))
        want[n] = jnp.where(lane == 0, first, jnp.where(lane == 1, second, 0))
    pl.semaphore_wait(barrier, PEERS)

    def tell(n):
        return pltpu.make_async_remote_copy(
            src_ref=want.at[n], dst_ref=got.at[n],
            send_sem=wsend.at[n], recv_sem=wrecv.at[n],
            device_id={"rows": peer(n, 1)}, device_id_type=MESH,
        )

    def start_tell(n, carry):
        tell(n).start()
        return carry

    def wait_tell(n, carry):
        tell(n).wait_recv()
        return carry

    lax.fori_loop(0, PEERS, start_tell, 0)
    loads[0].wait()
    for b in range(own):
        low[b] = rhs[b].astype(jnp.bfloat16)
    lax.fori_loop(0, PEERS, wait_tell, 0)
    asked_copy = pltpu.make_async_copy(got, got_smem, smem_sem.at[0])
    asked_copy.start()
    asked_copy.wait()

    def asked(n, k):
        return got_smem[n, 0, k]

    def entry(n, k, b):
        return entry_smem[b, n * CAP + k]

    def prepare():
        number = lax.broadcasted_iota(jnp.int32, (own, conds), 0) * conds
        number = number + lax.broadcasted_iota(jnp.int32, (own, conds), 1)
        column = lax.broadcasted_iota(jnp.int32, (own, 128), 1)
        table = jnp.full((own, 128), entries, jnp.int32)
        for n, (base, *locals_) in enumerate(chosen):
            for k, mine in enumerate(locals_):
                block = jnp.where(mine >= 0, base + mine, -2)
                found = jnp.where(ids[...] == block, number, entries)
                least = jnp.min(found, axis=1, keepdims=True)
                table = jnp.where(column == n * CAP + k, least, table)
        entry_rows[...] = table
        entry_copy = pltpu.make_async_copy(entry_rows, entry_smem, smem_sem.at[1])
        entry_copy.start()
        for rows_ref, full in ((alpha_rows, alpha), (beta_rows, beta)):
            spread = jnp.transpose(jnp.broadcast_to(rows_ref[0:1, :], (128, probes)))
            for part in range(points // 128):
                full[:, part * 128 : (part + 1) * 128] = spread
        cond[entries] = jnp.zeros(cond.shape[1:], cond.dtype)
        for load in loads[1:4]:
            load.wait()
        entry_copy.wait()

    def fetch(t, n):
        return pltpu.make_async_remote_copy(
            src_ref=pay.at[t, n], dst_ref=arr.at[t, n],
            send_sem=fsend.at[t, n], recv_sem=frecv.at[t, n],
            device_id={"rows": peer(n, -1)}, device_id_type=MESH,
        )

    def give(t, n):
        return pltpu.make_async_remote_copy(
            src_ref=ret.at[t, n], dst_ref=back.at[t, n],
            send_sem=bsend.at[t, n], recv_sem=brecv.at[t, n],
            device_id={"rows": peer(n, 1)}, device_id_type=MESH,
        )

    for t in range(ITERS):
        def send_low(n, carry):
            for k in range(CAP):
                pay[t, n, k] = low[jnp.maximum(asked(n, k), 0)]
            fetch(t, n).start()
            return carry

        lax.fori_loop(0, PEERS, send_low, 0)
        if t == 0:
            prepare()

        def own_forward(b, carry):
            total[b] = lax.dot_general(low[b], diag[b], NT, preferred_element_type=jnp.float32)
            return carry

        lax.fori_loop(0, own, own_forward, 0)
        if t == 0:
            loads[4].wait()

        def far_forward(n, carry):
            fetch(t, n).wait_recv()
            for b in range(own):
                acc = total[b]
                for k in range(CAP):
                    factor = cond[entry(n, k, b)]
                    acc = acc + lax.dot_general(
                        arr[t, n, k], factor, NT, preferred_element_type=jnp.float32
                    )
                total[b] = acc
            return carry

        lax.fori_loop(0, PEERS, far_forward, 0)
        for b in range(own):
            scaled[b] = (precision[b : b + 1, :] * total[b]).astype(jnp.bfloat16)

        def far_back(n, carry):
            for k in range(CAP):
                acc = jnp.zeros(total.shape[1:], jnp.float32)
                for b in range(own):
                    factor = cond[entry(n, k, b)]
                    acc = acc + lax.dot_general(
                        scaled[b], factor, NN, preferred_element_type=jnp.float32
                    )
                ret[t, n, k] = acc.astype(jnp.bfloat16)
            give(t, n).start()
            return carry

        lax.fori_loop(0, PEERS, far_back, 0)
        now = rhs if t == 0 else direc
        for b in range(own):
            image_out[b] = lax.dot_general(
                scaled[b], diag[b], NN, preferred_element_type=jnp.float32
            ) + hessian[b : b + 1, :] * now[b]

        def gather_back(n, carry):
            give(t, n).wait_recv()
            terms = [back[t, n, k].astype(jnp.float32) for k in range(CAP)]
            for b in range(own):
                acc = image_out[b]
                for k in range(CAP):
                    acc = acc + jnp.where(asked(n, k) == b, 1.0, 0.0) * terms[k]
                image_out[b] = acc
            return carry

        lax.fori_loop(0, PEERS, gather_back, 0)
        if t == 0:
            for b in range(own):
                left = rhs[b] - alpha[...] * image_out[b]
                res_out[b] = left
                new = left + beta[...] * rhs[b]
                direc[b] = new
                low[b] = new.astype(jnp.bfloat16)

    def drain(n, carry):
        tell(n).wait_send()
        for t in range(ITERS):
            fetch(t, n).wait_send()
            give(t, n).wait_send()
        return carry

    lax.fori_loop(0, PEERS, drain, 0)


def on_device(rhs, precision, hessian, diag_blocks, cond_blocks, cond_ids, step_alpha, step_beta):
    dev_count = lax.axis_size("rows")
    own, probes, points = rhs.shape
    conds = cond_ids.shape[1]
    entries = own * conds
    vmem = pl.BlockSpec(memory_space=pltpu.VMEM)
    hbm = pl.BlockSpec(memory_space=pl.ANY)
    low_type = jnp.bfloat16
    slots = (ITERS, PEERS, CAP, probes, points)
    res1, image1 = pl.pallas_call(
        functools.partial(kernel, dev_count),
        out_shape=[jax.ShapeDtypeStruct(rhs.shape, jnp.float32)] * 2,
        in_specs=[vmem] * 3 + [hbm] * 5,
        out_specs=[vmem, vmem],
        scratch_shapes=[
            pltpu.VMEM(rhs.shape, jnp.float32),
            pltpu.VMEM(precision.shape, jnp.float32),
            pltpu.VMEM(hessian.shape, jnp.float32),
            pltpu.VMEM(diag_blocks.shape, low_type),
            pltpu.VMEM((entries + 1, points, points), low_type),
            pltpu.VMEM(rhs.shape, low_type),
            pltpu.VMEM(rhs.shape, jnp.float32),
            pltpu.VMEM(rhs.shape, low_type),
            pltpu.VMEM(rhs.shape, jnp.float32),
            pltpu.VMEM((probes, points), jnp.float32),
            pltpu.VMEM((probes, points), jnp.float32),
            pltpu.VMEM((PEERS, 1, 128), jnp.int32),
            pltpu.VMEM((PEERS, 1, 128), jnp.int32),
            pltpu.VMEM((own, 128), jnp.int32),
            pltpu.SMEM((PEERS, 1, 128), jnp.int32),
            pltpu.SMEM((own, 128), jnp.int32),
            pltpu.VMEM(slots, low_type),
            pltpu.VMEM(slots, low_type),
            pltpu.VMEM(slots, low_type),
            pltpu.VMEM(slots, low_type),
            pltpu.SemaphoreType.DMA((5,)),
            pltpu.SemaphoreType.DMA((2,)),
            pltpu.SemaphoreType.DMA((PEERS,)),
            pltpu.SemaphoreType.DMA((PEERS,)),
            pltpu.SemaphoreType.DMA((ITERS, PEERS)),
            pltpu.SemaphoreType.DMA((ITERS, PEERS)),
            pltpu.SemaphoreType.DMA((ITERS, PEERS)),
            pltpu.SemaphoreType.DMA((ITERS, PEERS)),
        ],
        compiler_params=pltpu.CompilerParams(
            collective_id=0, has_side_effects=True, vmem_limit_bytes=40 * 1024 * 1024
        ),
    )(
        cond_ids, step_alpha, step_beta, rhs, precision, hessian, diag_blocks,
        cond_blocks.reshape(entries, points, points),
    )
    alpha0 = step_alpha[0][None, :, None]
    beta0 = step_beta[0][None, :, None]
    alpha1 = step_alpha[1][None, :, None]
    beta1 = step_beta[1][None, :, None]
    dir1 = res1 + beta0 * rhs
    sol = alpha0 * rhs + alpha1 * dir1
    res = res1 - alpha1 * image1
    return (sol, res, res + beta1 * dir1)


def solution(mesh):
    in_specs = (
        P(("groups", "rows"), None, None),
        P(("groups", "rows"), None),
        P(("groups", "rows"), None),
        P(("groups", "rows"), None, None),
        P(("groups", "rows"), None, None, None),
        P(("groups", "rows"), None),
        P(),
        P(),
    )
    out_specs = (
        P(("groups", "rows"), None, None),
        P(("groups", "rows"), None, None),
        P(("groups", "rows"), None, None),
    )
    return jax.shard_map(
        on_device, mesh=mesh, in_specs=in_specs, out_specs=out_specs, check_vma=False
    )
```
